32 devices in a mesh: groups: 2 (over y), dp: 4 (over z), mp: 4 (over x, core).
Axes of the slice: x: 2, y: 2, z: 4, core: 2. Of those that a mesh axis runs over, the one named last changes fastest.
Arguments:
- tile_rows: bfloat16 [128, 32, 1280], P(('groups', 'dp'), None, 'mp'), parts along dimension 0, may hold values from -6 to 6
- tile_count: int32 [128], P(('groups', 'dp')), parts along dimension 0, may hold values from 1 to 4, as said below
- tile_order: int32 [128], P(('groups', 'dp')), parts along dimension 0, may hold values from 0 to 3, as said below
- route: int32 [128, 1], P(('groups', 'dp')), parts along dimension 0, may hold values from 0 to 3; in each aligned block of 16 rows (0 to 15, 16 to 31, ...) at most 8 rows name the same one
- tile_embed: bfloat16 [16, 1280], P(None, 'mp'), may hold values from -3 to 3
- norm_gain: float32 [1280], replicated, may hold values from 0.5 to 2
- norm_bias: float32 [1280], replicated, may hold values from -3 to 3
- w_qkv: bfloat16 [1280, 3, 1280], P(None, None, 'mp'), may hold values from -3 to 3
- w_out: bfloat16 [1280, 1280], P('mp'), may hold values from -0.15625 to 0.15625
- w_proj: bfloat16 [1280, 8192], P(None, 'mp'), may hold values from -0.15625 to 0.15625
- w_kv: bfloat16 [8192, 2048], P('mp', 'dp'), may hold values from -0.0625 to 0.0625
- key_gain: float32 [128], replicated, may hold values from 0.5 to 2
Outputs:
- cross_kv: bfloat16 [256, 32, 2048], P(('groups', 'dp', 'mp')), parts along dimension 0
The draws below stay inside these ranges and needn't reach their ends.
There are 2 independent parts, one for each index of `groups`. The reference program is written for one: setup_inputs(seed, part) draws one part's arguments, and reference() takes and returns one part's arrays. A program takes and returns all parts, laid end to end along the dimension named above; an argument that names none is the same for every part. Nothing has to cross between parts.
Inputs may be any that keep to these rules, and one draw needn't show every extreme that they name: `tile_count`: tiles of one image stand in consecutive slots of one index of dp; the first image of every index of dp has 4 tiles, and the last may be cut at the end of its slots. `tile_order`: counts 0, 1 and so on along the tiles of one image. `route`: the 16 tiles of one index of dp name each destination at most 8 times; in some index of dp some destination is named exactly 8 times.
All inputs are finite; a program needn't handle non-finite values.
Results may differ from the reference program's by a relative error of at most 0.019.
Values may be sent and summed in bfloat16 or wider, within the bound.
A program may use at most 128 MiB of HBM per device.

```python
import math
import jax
import jax.numpy as jnp
import numpy as np
from jax import lax

D = 1280
HEADS = 16
HD = 80
DEC = 8192
KVD = 1024
DEC_HD = 128
MAXT = 4
P_SIZE = 32
TS = 16
PEERS = 4
CAP = 8
HL = 4
TILES = 64
SLOTS = 128
N_MP = 4


def request_layout(key):
    sizes_drawn = jax.random.randint(key, (PEERS, TS), 1, MAXT + 1)
    sizes_drawn = sizes_drawn.at[:, 0].set(MAXT)
    end_slot = jnp.cumsum(sizes_drawn, axis=1)
    start_slot = end_slot - sizes_drawn
    slot_ids = jnp.arange(TS)
    request_of = jnp.sum((slot_ids[None, :, None] >= end_slot[:, None, :]).astype(jnp.int32), axis=2)
    first_slot = jnp.take_along_axis(start_slot, request_of, axis=1)
    last_slot = jnp.minimum(jnp.take_along_axis(end_slot, request_of, axis=1), TS)
    return ((last_slot - first_slot).reshape(-1), (slot_ids[None, :] - first_slot).reshape(-1))


def draw_tile_count(key, part):
    layout = request_layout(key)
    return layout[0].astype(jnp.int32)


def draw_tile_order(key, part):
    layout = request_layout(key)
    return layout[1].astype(jnp.int32)


def draw_w_qkv(key, part):
    key = jax.random.fold_in(key, 7)
    first_key = jax.random.fold_in(key, 0)
    base = jax.random.truncated_normal(first_key, -4.0, 4.0, (D, 3, D), jnp.float32) / math.sqrt(D)
    return base.astype(jnp.bfloat16)


def block_levels(stream_key, dims, cuts, least, high):
    level, own = 1.0, jax.random.fold_in(stream_key, 6)
    for axis_at, parts in cuts:
        draws = jnp.exp(jax.random.uniform(jax.random.fold_in(own, axis_at), (parts,), jnp.float32, least / len(cuts), high / len(cuts)))
        level = level * jnp.repeat(draws, dims[axis_at] // parts).reshape([-1 if axis == axis_at else 1 for axis in range(len(dims))])
    return level


def routed_block(rng, own, number, rows, amount, top, most, slope):
    ranking = jax.random.permutation(rng, amount)
    packed, ordinary = load_shares(amount, rows * top, most, slope, True), load_shares(amount, rows * top, most, slope, False)
    places = jnp.arange(amount)

    def named(sizes, offset_by):
        used = int((sizes > 0).sum())
        fixed = max(1, used // 4)
        passed = fixed + (places - fixed + offset_by * (used - fixed)) % max(1, amount - fixed)
        return jnp.zeros((amount,), jnp.int32).at[ranking[jnp.where(places < fixed, places, passed)]].set(jnp.asarray(sizes, jnp.int32))

    sizes = jnp.where(number % 4 == 0, named(packed, number // 4), named(ordinary, number - number // 4 - 1))
    mixed = jax.random.permutation(jax.random.fold_in(own, 3), amount)
    donor, sink = mixed[0:amount // 2 * 2:2], mixed[1:amount // 2 * 2:2]
    room = jnp.minimum(sizes[donor] - 1, most - sizes[sink]) // 2
    room = jnp.where((donor == ranking[0]) | (sink == ranking[0]) | (sizes[sink] == 0), 0, jnp.maximum(room, 0))
    passed = jax.random.randint(jax.random.fold_in(own, 4), (amount // 2,), 0, 1 << 20) % (room + 1)
    sizes = sizes.at[donor].add(-passed).at[sink].add(passed)
    items = jnp.searchsorted(jnp.cumsum(sizes), jnp.arange(rows * top), side="right").astype(jnp.int32)
    grid = items.reshape(top, rows).T
    grid = grid[jax.random.permutation(jax.random.fold_in(own, 1), rows)]
    offset_by = jax.random.randint(jax.random.fold_in(own, 2), (rows, 1), 0, top)
    return jnp.take_along_axis(grid, (jnp.arange(top)[None, :] + offset_by) % top, axis=1)


def load_shares(amount, total, bound, skew, full):
    weights = [(1 << 20) // math.isqrt(standing ** skew) + 1 for standing in range(1, amount + 1)]
    largest = bound if full else min(bound, max(-(-total // amount), total * weights[0] // sum(weights)))
    least = 1 if total - largest >= amount - 1 else 0
    given, surplus = [largest] + [least] * (amount - 1), total - largest - least * (amount - 1)
    while surplus > 0:
        free = [i for i in range(1, amount) if given[i] < largest] or [i for i in range(1, amount) if given[i] < bound]
        mass, left = sum([weights[i] for i in free]), surplus
        for i in free:
            extra = min(bound - given[i], max(1, left * weights[i] // mass), surplus)
            given[i] = given[i] + extra
            surplus = surplus - extra
    return np.array(given)


def scatter_about(own_key, shape, spread, reach, cuts=(), dtype=jnp.bfloat16):
    level = block_levels(own_key, shape, cuts, -0.22, 0.18) if cuts else 1.0
    values = jax.random.normal(own_key, shape, jnp.float32) * spread * level
    return jnp.minimum(jnp.maximum(values, -reach), reach).astype(dtype)


def setup_inputs(seed: int = 0, part: int = 0) -> dict:
    streams_of = jax.random.split(jax.random.key(seed), 13)
    part_keys = jax.random.split(jax.random.fold_in(streams_of[12], part), 13)
    tile_rows = scatter_about(part_keys[0], (TILES, P_SIZE, D), 1.0, 6.0, ((0, 4), (2, 4)))
    tile_count = draw_tile_count(jax.random.fold_in(jax.random.fold_in(streams_of[12], part), 71), part)
    tile_order = draw_tile_order(jax.random.fold_in(jax.random.fold_in(streams_of[12], part), 71), part)
    route_keys = jax.random.split(jax.random.fold_in(part_keys[3], 1), TILES // TS)
    route_turns = jax.random.permutation(jax.random.fold_in(part_keys[3], 3), TILES // TS)
    route = jax.vmap(lambda own, number: routed_block(jax.random.fold_in(part_keys[3], 2), own, number, TS, PEERS, 1, CAP, 2))(route_keys, route_turns).reshape((TILES, 1))
    tile_embed = scatter_about(streams_of[4], (MAXT * MAXT, D), 0.5, 3.0, ((1, 4),))
    norm_gain = jnp.clip(jnp.exp(jax.random.uniform(streams_of[5], (D,), jnp.float32, math.log(0.5), math.log(2.0))), 0.5, 2.0)
    norm_bias = scatter_about(streams_of[6], (D,), 0.5, 3.0, (), jnp.float32)
    w_qkv = draw_w_qkv(jax.random.fold_in(streams_of[12], 71), part)
    w_out = scatter_about(streams_of[8], (D, D), D ** -0.5, 0.15625, ((0, 4),))
    w_proj = scatter_about(streams_of[9], (D, DEC), D ** -0.5, 0.15625, ((1, 4),))
    w_kv = scatter_about(streams_of[10], (DEC, 2 * KVD), DEC ** -0.5, 0.0625, ((0, 4), (1, 4)))
    key_gain = jnp.clip(jnp.exp(jax.random.uniform(streams_of[11], (DEC_HD,), jnp.float32, math.log(0.5), math.log(2.0))), 0.5, 2.0)
    return dict(tile_rows=tile_rows, tile_count=tile_count, tile_order=tile_order, route=route, tile_embed=tile_embed, norm_gain=norm_gain, norm_bias=norm_bias, w_qkv=w_qkv, w_out=w_out, w_proj=w_proj, w_kv=w_kv, key_gain=key_gain)


def layer_norm(values, gain, bias):
    row_mean = lax.optimization_barrier(jnp.mean(values, axis=-1, keepdims=True))
    centred = values - row_mean
    row_var = lax.optimization_barrier(jnp.mean(centred * centred, axis=-1, keepdims=True))
    return centred * lax.rsqrt(row_var + 1e-05) * gain + bias

def reference(tile_rows, tile_count, tile_order, route, tile_embed, norm_gain, norm_bias, w_qkv, w_out, w_proj, w_kv, key_gain):
    lookup = ((tile_count - 1) * MAXT + tile_order).astype(jnp.int32)
    table_rows = tile_embed[lookup].astype(jnp.float32)
    embedded = (tile_rows.astype(jnp.float32) + table_rows[:, None, :]).astype(jnp.bfloat16)
    normed = layer_norm(embedded.astype(jnp.float32), norm_gain, norm_bias).astype(jnp.bfloat16)
    qkv = jnp.einsum('tpd,dce->tpce', normed.astype(jnp.float32), w_qkv.astype(jnp.float32)).astype(jnp.bfloat16)
    split_qkv = qkv.reshape(TILES, P_SIZE, 3, HEADS, HD)
    queries = split_qkv[:, :, 0].astype(jnp.float32)
    keys_all = split_qkv[:, :, 1].astype(jnp.float32)
    values_all = split_qkv[:, :, 2].astype(jnp.float32)
    scores = jnp.einsum('tqhe,tkhe->thqk', queries, keys_all) / math.sqrt(HD)
    weights = jax.nn.softmax(scores, axis=-1).astype(jnp.bfloat16)
    context = jnp.einsum('thqk,tkhe->tqhe', weights.astype(jnp.float32), values_all).astype(jnp.bfloat16)
    context = context.reshape(TILES * P_SIZE, N_MP, HL * HD)
    out_rows = w_out.reshape(N_MP, HL * HD, D)
    attended = jnp.zeros((TILES * P_SIZE, D), jnp.float32)
    for group in range(N_MP):
        term = jnp.dot(context[:, group], out_rows[group], preferred_element_type=jnp.float32)
        attended = attended + lax.optimization_barrier(term.astype(jnp.bfloat16)).astype(jnp.float32)
    encoded = (embedded.reshape(TILES * P_SIZE, D).astype(jnp.float32) + attended).astype(jnp.bfloat16)
    vision = jnp.dot(encoded, w_proj, preferred_element_type=jnp.float32).astype(jnp.bfloat16)
    group_width = DEC // N_MP
    projected = jnp.zeros((TILES * P_SIZE, 2 * KVD), jnp.float32)
    for group in range(N_MP):
        term = jnp.dot(vision[:, group * group_width:(group + 1) * group_width], w_kv[group * group_width:(group + 1) * group_width], preferred_element_type=jnp.float32)
        projected = projected + lax.optimization_barrier(term.astype(jnp.bfloat16)).astype(jnp.float32)
    key_part = projected[:, :KVD].reshape(TILES * P_SIZE, KVD // DEC_HD, DEC_HD)
    key_scale = lax.rsqrt(lax.optimization_barrier(jnp.mean(key_part * key_part, axis=-1, keepdims=True)) + 1e-06)
    key_part = (key_part * key_scale * key_gain).reshape(TILES * P_SIZE, KVD)
    combined = jnp.concatenate([key_part, projected[:, KVD:]], axis=1).astype(jnp.bfloat16)
    combined = combined.reshape(TILES, P_SIZE, 2 * KVD)
    target = route[:, 0].astype(jnp.int32)
    source = (jnp.arange(TILES) // TS).astype(jnp.int32)
    target_hot = (target[:, None] == jnp.arange(PEERS)[None, :]).astype(jnp.int32).reshape(PEERS, TS, PEERS)
    earlier = jnp.cumsum(target_hot, axis=1) - target_hot
    position = lax.optimization_barrier(jnp.sum(earlier * target_hot, axis=2)).reshape(TILES).astype(jnp.int32)
    out_index = (target * (PEERS * CAP) + source * CAP + position).astype(jnp.int32)
    cross_kv = jnp.zeros((SLOTS, P_SIZE, 2 * KVD), jnp.bfloat16).at[out_index].set(combined)
    return cross_kv
```

```python
import math

import jax
import jax.numpy as jnp
from jax import lax
from jax.sharding import PartitionSpec as P

HD = 80
KVD = 1024
DEC_HD = 128
MAXT = 4


def per_device(
    tile_rows,
    tile_count,
    tile_order,
    route,
    tile_embed,
    norm_gain,
    norm_bias,
    w_qkv,
    w_out,
    w_proj,
    w_kv,
    key_gain,
):
    tiles, patches, local_width = tile_rows.shape
    peers = lax.axis_size("dp")
    models = lax.axis_size("mp")
    cap = 2 * tiles // peers
    f32, bf16 = jnp.float32, jnp.bfloat16

    part = lax.dot_general(w_kv, w_proj, (((0,), (1,)), ((), ())), preferred_element_type=f32)
    part = lax.psum_scatter(part.astype(bf16), "mp", scatter_dimension=0, tiled=True)
    w_all = lax.all_gather(part, ("dp", "mp"), axis=0, tiled=True)
    out_all = lax.all_gather(w_out, "mp", axis=0, tiled=True)

    lookup = (tile_count - 1) * MAXT + tile_order
    lookup_hot = (lookup[:, None] == jnp.arange(MAXT * MAXT)[None, :]).astype(bf16)
    table_rows = jnp.dot(lookup_hot, tile_embed, preferred_element_type=f32)
    embedded = (tile_rows.astype(f32) + table_rows[:, None, :]).astype(bf16)
    full_rows = lax.all_gather(
        embedded.reshape(tiles * patches, local_width), "mp", axis=1, tiled=True
    )
    full_float = full_rows.astype(f32)
    row_mean = jnp.mean(full_float, axis=-1, keepdims=True)
    centred = full_float - row_mean
    row_var = jnp.mean(centred * centred, axis=-1, keepdims=True)
    normed = (centred * lax.rsqrt(row_var + 1e-05) * norm_gain + norm_bias).astype(bf16)
    width = full_rows.shape[1]
    head_width = w_qkv.shape[2]
    heads = head_width // HD
    qkv = jnp.dot(
        normed, w_qkv.reshape(width, 3 * head_width), preferred_element_type=f32
    ).astype(bf16)
    qkv = qkv.reshape(tiles, patches, 3, heads, HD)
    scores = jnp.einsum(
        "sqhe,skhe->shqk", qkv[:, :, 0], qkv[:, :, 1], preferred_element_type=f32
    ) / math.sqrt(HD)
    weights = jax.nn.softmax(scores, axis=-1).astype(bf16)
    context = jnp.einsum(
        "shqk,skhe->sqhe", weights, qkv[:, :, 2], preferred_element_type=f32
    ).astype(bf16)

    destination = route[:, 0]
    dest_hot = (destination[:, None] == jnp.arange(peers)[None, :]).astype(jnp.int32)
    earlier = jnp.cumsum(dest_hot, axis=0) - dest_hot
    position = jnp.sum(earlier * dest_hot, axis=1)
    target = destination * cap + position
    placing = target[:, None] == jnp.arange(peers * cap)[None, :]
    place_t = placing.astype(bf16).T
    occupied = jnp.sum(placing.astype(jnp.int32), axis=0).reshape(peers, 1, cap)
    occupied = jnp.broadcast_to(occupied, (peers, 1, cap))

    def send(values):
        rows = jnp.dot(
            place_t, values.reshape(tiles, patches * local_width), preferred_element_type=f32
        ).astype(bf16).reshape(peers, cap, patches * local_width)
        rows = lax.all_to_all(rows, "dp", split_axis=0, concat_axis=0, tiled=True)
        rows = lax.all_to_all(rows, "mp", split_axis=0, concat_axis=0, tiled=True)
        rows = rows.reshape(models, cap * patches, local_width)
        return rows.transpose(1, 0, 2).reshape(cap * patches, models * local_width)

    filled = lax.all_to_all(occupied, "dp", split_axis=0, concat_axis=0, tiled=True)
    used = lax.dynamic_index_in_dim(filled, lax.axis_index("mp"), 0, keepdims=False)[0] > 0
    ctx = send(context)
    emb = send(embedded)
    attended = jnp.dot(ctx, out_all, preferred_element_type=f32)
    encoded = (emb.astype(f32) + attended).astype(bf16)
    projected = lax.dot_general(
        encoded, w_all, (((1,), (1,)), ((), ())), preferred_element_type=f32
    )
    rows = cap * patches
    key_part = projected[:, :KVD].reshape(rows, KVD // DEC_HD, DEC_HD)
    key_scale = lax.rsqrt(jnp.mean(key_part * key_part, axis=-1, keepdims=True) + 1e-06)
    key_part = (key_part * key_scale * key_gain).reshape(rows, KVD)
    finished = jnp.concatenate([key_part, projected[:, KVD:]], axis=1)
    finished = finished.reshape(cap, patches, projected.shape[1])
    finished = jnp.where(used[:, None, None], finished, 0.0)
    return finished.astype(bf16)


def solution(mesh):
    return jax.shard_map(
        per_device,
        mesh=mesh,
        in_specs=(
            P(("groups", "dp"), None, "mp"),
            P(("groups", "dp")),
            P(("groups", "dp")),
            P(("groups", "dp"), None),
            P(None, "mp"),
            P(),
            P(),
            P(None, None, "mp"),
            P("mp", None),
            P(None, "mp"),
            P("mp", "dp"),
            P(),
        ),
        out_specs=P(("groups", "dp", "mp"), None, None),
        check_vma=False,
    )
```

```python
import math

import jax
import jax.numpy as jnp
import numpy as np
from jax import lax
from jax.experimental import pallas as pl
from jax.experimental.pallas import tpu as pltpu
from jax.sharding import PartitionSpec as P

HD = 80
KVD = 1024
DEC_HD = 128
MAXT = 4


def per_device(
    tile_rows,
    tile_count,
    tile_order,
    route,
    tile_embed,
    norm_gain,
    norm_bias,
    w_qkv,
    w_out,
    w_proj,
    w_kv,
    key_gain,
):
    tiles, patches, local_width = tile_rows.shape
    peers = lax.axis_size("dp")
    models = lax.axis_size("mp")
    cap = 2 * tiles // peers
    f32, bf16 = jnp.float32, jnp.bfloat16

    part = lax.dot_general(w_kv, w_proj, (((0,), (1,)), ((), ())), preferred_element_type=f32)
    part = lax.psum_scatter(part.astype(bf16), "mp", scatter_dimension=0, tiled=True)
    w_all = lax.all_gather(part, ("dp", "mp"), axis=0, tiled=True)
    out_all = lax.all_gather(w_out, "mp", axis=0, tiled=True)

    lookup = (tile_count - 1) * MAXT + tile_order
    lookup_hot = (lookup[:, None] == jnp.arange(MAXT * MAXT)[None, :]).astype(bf16)
    table_rows = jnp.dot(lookup_hot, tile_embed, preferred_element_type=f32)
    embedded = (tile_rows.astype(f32) + table_rows[:, None, :]).astype(bf16)
    full_rows = lax.all_gather(
        embedded.reshape(tiles * patches, local_width), "mp", axis=1, tiled=True
    )
    full_float = full_rows.astype(f32)
    row_mean = jnp.mean(full_float, axis=-1, keepdims=True)
    centred = full_float - row_mean
    row_var = jnp.mean(centred * centred, axis=-1, keepdims=True)
    normed = (centred * lax.rsqrt(row_var + 1e-05) * norm_gain + norm_bias).astype(bf16)
    width = full_rows.shape[1]
    head_width = w_qkv.shape[2]
    heads = head_width // HD
    qkv = jnp.dot(
        normed, w_qkv.reshape(width, 3 * head_width), preferred_element_type=f32
    ).astype(bf16)
    qkv = qkv.reshape(tiles, patches, 3, heads, HD)
    scores = jnp.einsum(
        "sqhe,skhe->shqk", qkv[:, :, 0], qkv[:, :, 1], preferred_element_type=f32
    ) / math.sqrt(HD)
    weights = jax.nn.softmax(scores, axis=-1).astype(bf16)
    context = jnp.einsum(
        "shqk,skhe->sqhe", weights, qkv[:, :, 2], preferred_element_type=f32
    ).astype(bf16)

    destination = route[:, 0]
    dest_hot = (destination[:, None] == jnp.arange(peers)[None, :]).astype(jnp.int32)
    earlier = jnp.cumsum(dest_hot, axis=0) - dest_hot
    position = jnp.sum(earlier * dest_hot, axis=1)
    target = destination * cap + position
    placing = target[:, None] == jnp.arange(peers * cap)[None, :]
    place_t = placing.astype(bf16).T
    occupied = jnp.sum(placing.astype(jnp.int32), axis=0).reshape(peers, 1, cap)
    occupied = jnp.broadcast_to(occupied, (peers, 1, cap))

    def send(values):
        rows = jnp.dot(
            place_t, values.reshape(tiles, patches * local_width), preferred_element_type=f32
        ).astype(bf16).reshape(peers, cap, patches * local_width)
        rows = lax.all_to_all(rows, "dp", split_axis=0, concat_axis=0, tiled=True)
        rows = lax.all_to_all(rows, "mp", split_axis=0, concat_axis=0, tiled=True)
        rows = rows.reshape(models, cap * patches, local_width)
        return rows.transpose(1, 0, 2).reshape(cap * patches, models * local_width)

    filled = lax.all_to_all(occupied, "dp", split_axis=0, concat_axis=0, tiled=True)
    used = lax.dynamic_index_in_dim(filled, lax.axis_index("mp"), 0, keepdims=False)[0] > 0
    ctx = send(context)
    emb = send(embedded)
    attended = jnp.dot(ctx, out_all, preferred_element_type=f32)
    encoded = (emb.astype(f32) + attended).astype(bf16)
    projected = lax.dot_general(
        encoded, w_all, (((1,), (1,)), ((), ())), preferred_element_type=f32
    )
    rows = cap * patches
    key_part = projected[:, :KVD].reshape(rows, KVD // DEC_HD, DEC_HD)
    key_scale = lax.rsqrt(jnp.mean(key_part * key_part, axis=-1, keepdims=True) + 1e-06)
    key_part = (key_part * key_scale * key_gain).reshape(rows, KVD)
    finished = jnp.concatenate([key_part, projected[:, KVD:]], axis=1)
    finished = finished.reshape(cap, patches, projected.shape[1])
    finished = jnp.where(used[:, None, None], finished, 0.0)
    return finished.astype(bf16)


N = 4
MESH = pl.DeviceIdType.MESH


def selector():
    table = np.zeros((N * HD, N * 128), np.float32)
    for head in range(N):
        for e in range(HD):
            table[head * HD + e, head * 128 + e] = 1.0
    return table


def kernel(
    emb_ref, tgt_ref, gain_ref, bias_ref, wqkv_ref, wout_ref, wproj_ref, wkv_ref, kgain_ref,
    sel_ref, selt_ref, out_ref,
    embf, ctxs, csend, esend, ctxr, embr, woutf, rssrc, rsbuf, own, wall,
    es, er, os, orr, rs_s, rs_r, zs, zr, ys, yr, xs, xr, c_s, c_r, cs, cr, ms, mr,
):
    f32, bf16 = jnp.float32, jnp.bfloat16
    g, j, m = lax.axis_index("groups"), lax.axis_index("dp"), lax.axis_index("mp")
    xp = lax.rem(m + 2, N)
    cp = m + 1 - 2 * lax.rem(m, 2)
    xcp = lax.rem(cp + 2, N)
    rows, lanes = emb_ref.shape
    blk = wqkv_ref.shape[2]
    slots = ctxr.shape[1]
    half = wall.shape[3]

    def copy(src, dst, ssem, rsem, dev):
        return pltpu.make_async_remote_copy(
            src_ref=src, dst_ref=dst, send_sem=ssem, recv_sem=rsem,
            device_id=dev, device_id_type=MESH,
        )

    barrier = pltpu.get_barrier_semaphore()
    for k in range(1, N * N):
        other = lax.rem(j * N + m + k, N * N)
        pl.semaphore_signal(
            barrier, inc=1, device_id=(g, other // N, lax.rem(other, N)), device_id_type=MESH
        )
    pl.semaphore_signal(barrier, inc=1, device_id=(1 - g, j, m), device_id_type=MESH)
    pl.semaphore_wait(barrier, N * N)

    pending = []

    def start(c):
        c.start()
        pending.append(c)

    start(copy(emb_ref, embf.at[m], es.at[0], er.at[m], (g, j, xp)))
    start(copy(emb_ref, embf.at[m], es.at[1], er.at[m], (g, j, cp)))

    cols = pl.ds(pl.multiple_of(g * half, half), half)
    for k in (2, 3, 1, 0):
        to = lax.rem(m + k, N)
        prod = jnp.dot(
            wproj_ref[pl.ds(pl.multiple_of(to * blk, 16), blk), :], wkv_ref[:, cols],
            preferred_element_type=f32,
        )
        if k == 0:
            own[...] = prod
        else:
            rssrc[k] = prod.astype(bf16)
            start(copy(rssrc.at[k], rsbuf.at[m], rs_s.at[k], rs_r.at[m], (g, j, to)))

    emb_own = emb_ref[...]
    embf[m] = emb_own
    tgt = tgt_ref[...]
    place = lax.broadcasted_iota(jnp.int32, (slots, rows), 0)

    def routed(values, send, recv, ssem, rsem):
        for d in range(N):
            hot = (place + d * slots == tgt).astype(f32).astype(bf16)
            send[d] = jnp.dot(hot, values, preferred_element_type=f32).astype(bf16)
            here = jnp.logical_and(j == d, m == d)

            @pl.when(here)
            def _():
                recv[m] = send[d]

            @pl.when(jnp.logical_not(here))
            def _():
                copy(send.at[d], recv.at[m], ssem.at[d], rsem.at[m], (g, d, j)).start()

    def routed_arrived(send, recv, ssem, rsem):
        for k in range(N):
            @pl.when(jnp.logical_not(jnp.logical_and(j == m, m == k)))
            def _():
                copy(send.at[k], recv.at[k], ssem.at[k], rsem.at[k], (g, j, xp)).wait_recv()

    def routed_sent(send, recv, ssem, rsem):
        for d in range(N):
            @pl.when(jnp.logical_not(jnp.logical_and(j == d, m == d)))
            def _():
                copy(send.at[d], recv.at[m], ssem.at[d], rsem.at[m], (g, d, j)).wait_send()

    copy(emb_ref, embf.at[xp], es.at[0], er.at[xp], (g, j, xp)).wait_recv()
    start(copy(embf.at[xp], embf.at[xp], es.at[2], er.at[xp], (g, j, cp)))

    total = own[...]
    for k in (1, 3, 2):
        frm = lax.rem(m + k, N)
        copy(rssrc.at[k], rsbuf.at[frm], rs_s.at[k], rs_r.at[frm], (g, j, frm)).wait_recv()
        total = total + rsbuf[frm].astype(f32)
    mine = pl.ds(pl.multiple_of(m * blk, 16), blk)
    xrow = pl.ds(pl.multiple_of(xp * blk, 16), blk)
    crow = pl.ds(pl.multiple_of(cp * blk, 16), blk)
    xcrow = pl.ds(pl.multiple_of(xcp * blk, 16), blk)
    wall[g, j, mine, :] = total.astype(bf16)
    unit = wall.at[g, j, mine, :]
    for k in (1, 3, 2):
        start(copy(unit, unit, zs.at[k], zr.at[j], (g, lax.rem(j + k, N), m)))

    def spread(gg, jj, at):
        u = wall.at[gg, jj, mine, :]
        start(copy(u, u, xs.at[at], xr.at[gg, jj], (g, j, xp)))
        start(copy(u, u, c_s.at[at], c_r.at[gg, jj], (g, j, cp)))

    start(copy(unit, unit, ys.at[0], yr.at[j], (1 - g, j, m)))

    for b in (cp, xcp):
        copy(emb_ref, embf.at[b], es.at[0], er.at[b], (g, j, xp)).wait_recv()

    tile = rows // 16
    step = 4 * tile
    rid = lax.broadcasted_iota(jnp.int32, (step, step), 0) // tile
    cid = lax.broadcasted_iota(jnp.int32, (step, step), 1) // tile
    same = rid == cid

    def encode(r, carry):
        at = pl.ds(pl.multiple_of(r * step, step), step)
        x = [embf[n, at, :][:, :blk].astype(f32) for n in range(N)]
        mean = sum(jnp.sum(v, axis=-1, keepdims=True) for v in x) / (N * blk)
        x = [v - mean for v in x]
        var = sum(jnp.sum(v * v, axis=-1, keepdims=True) for v in x) / (N * blk)
        inv = lax.rsqrt(var + 1e-05)
        x = [(x[n] * inv * gain_ref[n] + bias_ref[n]).astype(bf16) for n in range(N)]
        parts = []
        for k in range(3):
            acc = jnp.zeros((step, blk), f32)
            for n in range(N):
                acc = acc + jnp.dot(
                    x[n], wqkv_ref[k, n * blk:(n + 1) * blk, :], preferred_element_type=f32
                )
            parts.append(
                jnp.dot(acc.astype(bf16), sel_ref[...], preferred_element_type=f32).astype(bf16)
            )
        ctx = jnp.zeros((step, blk), f32)
        for h in range(N):
            hs = slice(h * 128, (h + 1) * 128)
            scores = lax.dot_general(
                parts[0][:, hs], parts[1][:, hs], (((1,), (1,)), ((), ())),
                preferred_element_type=f32,
            ) / math.sqrt(HD)
            scores = jnp.where(same, scores, -1e30)
            top = jnp.max(scores, axis=-1, keepdims=True)
            e = jnp.where(same, jnp.exp(scores - top), 0.0)
            wts = (e / jnp.sum(e, axis=-1, keepdims=True)).astype(bf16)
            c = jnp.dot(wts, parts[2][:, hs], preferred_element_type=f32).astype(bf16)
            ctx = ctx + jnp.dot(c, selt_ref[h * 128:(h + 1) * 128, :], preferred_element_type=f32)
        ctxs[at, :] = ctx.astype(bf16)
        return carry

    lax.fori_loop(0, rows // step, encode, 0)
    routed(ctxs[...], csend, ctxr, cs, cr)
    routed(emb_own, esend, embr, ms, mr)

    start(copy(wout_ref, woutf.at[m], os.at[0], orr.at[m], (g, j, xp)))
    start(copy(wout_ref, woutf.at[m], os.at[1], orr.at[m], (g, j, cp)))
    woutf[m] = wout_ref[...]
    order = [0, 1, 3, 2]
    spread(g, j, 0)
    for k in order[1:]:
        jj = lax.rem(j + k, N)
        u = wall.at[g, jj, mine, :]
        copy(u, u, zs.at[k], zr.at[jj], (g, j, xp)).wait_recv()
        start(copy(u, u, ys.at[k], yr.at[jj], (1 - g, j, m)))
        spread(g, jj, k)
    for k in order:
        jj = lax.rem(j + k, N)
        u = wall.at[1 - g, jj, mine, :]
        copy(u, u, ys.at[k], yr.at[jj], (1 - g, j, m)).wait_recv()
        spread(1 - g, jj, N + k)
    copy(wout_ref, woutf.at[xp], os.at[0], orr.at[xp], (g, j, xp)).wait_recv()
    start(copy(woutf.at[xp], woutf.at[xp], os.at[2], orr.at[xp], (g, j, cp)))
    units = [(gg, k) for gg in range(2) for k in order]
    for gg, k in units:
        ga = g if gg == 0 else 1 - g
        jj = lax.rem(j + k, N)
        u = wall.at[ga, jj, xrow, :]
        copy(u, u, xs.at[gg * N + k], xr.at[ga, jj], (g, j, xp)).wait_recv()
        start(copy(u, u, c_s.at[8 + gg * N + k], c_r.at[2 + ga, jj], (g, j, cp)))

    routed_arrived(csend, ctxr, cs, cr)
    routed_arrived(esend, embr, ms, mr)
    for b in (cp, xcp):
        copy(wout_ref, woutf.at[b], os.at[0], orr.at[b], (g, j, xp)).wait_recv()
    enc = []
    for n in range(N):
        acc = jnp.zeros((slots, blk), f32)
        for k in range(N):
            acc = acc + jnp.dot(ctxr[k], woutf[k, n], preferred_element_type=f32)
        enc.append((embr[n][:, :blk].astype(f32) + acc).astype(bf16))
    used = embr[0][:, blk:blk + 1].astype(f32) > 0.5

    for gg, k in units:
        ga = g if gg == 0 else 1 - g
        jj = lax.rem(j + k, N)
        for b, row in ((0, crow), (2, xcrow)):
            u = wall.at[ga, jj, row, :]
            copy(u, u, c_s.at[0], c_r.at[b + ga, jj], (g, j, cp)).wait_recv()
        acc = jnp.zeros((slots, half), f32)
        for n in range(N):
            acc = acc + jnp.dot(
                enc[n], wall[ga, jj, n * blk:(n + 1) * blk, :], preferred_element_type=f32
            )
        key = (2 * jj + ga) * half < KVD
        for s in range(half // DEC_HD):
            p = acc[:, s * DEC_HD:(s + 1) * DEC_HD]
            scale = lax.rsqrt(jnp.mean(p * p, axis=-1, keepdims=True) + 1e-06)
            p = jnp.where(key, p * scale * kgain_ref[...], p)
            p = jnp.where(used, p, 0.0).astype(bf16)
            at = pl.ds(pl.multiple_of((2 * jj + ga) * half + s * DEC_HD, DEC_HD), DEC_HD)
            out_ref[:, at] = p

    for c in pending:
        c.wait_send()
    routed_sent(csend, ctxr, cs, cr)
    routed_sent(esend, embr, ms, mr)


def per_device_kernel(
    tile_rows, tile_count, tile_order, route, tile_embed, norm_gain, norm_bias,
    w_qkv, w_out, w_proj, w_kv, key_gain,
):
    f32, bf16 = jnp.float32, jnp.bfloat16
    tiles, patches, blk = tile_rows.shape
    cap = 2 * tiles // N
    rows, slots = tiles * patches, cap * patches
    width, columns = w_proj.shape[0], w_kv.shape[1] * N
    half = w_kv.shape[1] // 2
    lanes = -(-(blk + 1) // 128) * 128
    lookup = (tile_count - 1) * MAXT + tile_order
    lookup_hot = (lookup[:, None] == jnp.arange(MAXT * MAXT)[None, :]).astype(bf16)
    table_rows = jnp.dot(lookup_hot, tile_embed, preferred_element_type=f32)
    emb = (tile_rows.astype(f32) + table_rows[:, None, :]).astype(bf16).reshape(rows, blk)
    emb = jnp.pad(emb, ((0, 0), (0, lanes - blk)), constant_values=1)
    destination = route[:, 0]
    dest_hot = (destination[:, None] == jnp.arange(N)[None, :]).astype(jnp.int32)
    earlier = jnp.cumsum(dest_hot, axis=0) - dest_hot
    target = destination * cap + jnp.sum(earlier * dest_hot, axis=1)
    tgt = (target[:, None] * patches + jnp.arange(patches)[None, :]).reshape(1, rows)
    wqkv = w_qkv.transpose(1, 0, 2)
    wout = w_out.reshape(blk, N, blk).transpose(1, 0, 2)
    sel = jnp.asarray(selector(), bf16)
    selt = jnp.asarray(selector().T, bf16)
    vm = pl.BlockSpec(memory_space=pltpu.VMEM)
    sem = pltpu.SemaphoreType.DMA
    out = pl.pallas_call(
        kernel,
        out_shape=jax.ShapeDtypeStruct((slots, columns), bf16),
        in_specs=[vm] * 11,
        out_specs=vm,
        scratch_shapes=[
            pltpu.VMEM((N, rows, lanes), bf16),
            pltpu.VMEM((rows, blk), bf16),
            pltpu.VMEM((N, slots, blk), bf16),
            pltpu.VMEM((N, slots, lanes), bf16),
            pltpu.VMEM((N, slots, blk), bf16),
            pltpu.VMEM((N, slots, lanes), bf16),
            pltpu.VMEM((N, N, blk, blk), bf16),
            pltpu.VMEM((N, blk, half), bf16),
            pltpu.VMEM((N, blk, half), bf16),
            pltpu.VMEM((blk, half), f32),
            pltpu.VMEM((2, N, width, half), bf16),
            sem((3,)), sem((N,)), sem((3,)), sem((N,)),
            sem((N,)), sem((N,)), sem((N,)), sem((N,)), sem((N,)), sem((N,)),
            sem((2 * N,)), sem((2, N)), sem((4 * N,)), sem((4, N)),
            sem((N,)), sem((N,)), sem((N,)), sem((N,)),
        ],
        compiler_params=pltpu.CompilerParams(
            collective_id=0, has_side_effects=True, vmem_limit_bytes=56 << 20
        ),
    )(
        emb, tgt, norm_gain.reshape(N, 1, blk), norm_bias.reshape(N, 1, blk), wqkv, wout,
        w_proj, w_kv, key_gain.reshape(1, -1), sel, selt,
    )
    return out.reshape(cap, patches, columns)


def solution(mesh):
    aligned = mesh.shape["dp"] == N and mesh.shape["mp"] == N and mesh.shape["groups"] == 2
    return jax.shard_map(
        per_device_kernel if aligned else per_device,
        mesh=mesh,
        in_specs=(
            P(("groups", "dp"), None, "mp"),
            P(("groups", "dp")),
            P(("groups", "dp")),
            P(("groups", "dp"), None),
            P(None, "mp"),
            P(),
            P(),
            P(None, None, "mp"),
            P("mp", None),
            P(None, "mp"),
            P("mp", "dp"),
            P(),
        ),
        out_specs=P(("groups", "dp", "mp"), None, None),
        check_vma=False,
    )
```

```python
import math

import jax
import jax.numpy as jnp
import numpy as np
from jax import lax
from jax.experimental import pallas as pl
from jax.experimental.pallas import tpu as pltpu
from jax.sharding import PartitionSpec as P

HD = 80
KVD = 1024
DEC_HD = 128
MAXT = 4


def per_device(
    tile_rows,
    tile_count,
    tile_order,
    route,
    tile_embed,
    norm_gain,
    norm_bias,
    w_qkv,
    w_out,
    w_proj,
    w_kv,
    key_gain,
):
    tiles, patches, local_width = tile_rows.shape
    peers = lax.axis_size("dp")
    models = lax.axis_size("mp")
    cap = 2 * tiles // peers
    f32, bf16 = jnp.float32, jnp.bfloat16

    part = lax.dot_general(w_kv, w_proj, (((0,), (1,)), ((), ())), preferred_element_type=f32)
    part = lax.psum_scatter(part.astype(bf16), "mp", scatter_dimension=0, tiled=True)
    w_all = lax.all_gather(part, ("dp", "mp"), axis=0, tiled=True)
    out_all = lax.all_gather(w_out, "mp", axis=0, tiled=True)

    lookup = (tile_count - 1) * MAXT + tile_order
    lookup_hot = (lookup[:, None] == jnp.arange(MAXT * MAXT)[None, :]).astype(bf16)
    table_rows = jnp.dot(lookup_hot, tile_embed, preferred_element_type=f32)
    embedded = (tile_rows.astype(f32) + table_rows[:, None, :]).astype(bf16)
    full_rows = lax.all_gather(
        embedded.reshape(tiles * patches, local_width), "mp", axis=1, tiled=True
    )
    full_float = full_rows.astype(f32)
    row_mean = jnp.mean(full_float, axis=-1, keepdims=True)
    centred = full_float - row_mean
    row_var = jnp.mean(centred * centred, axis=-1, keepdims=True)
    normed = (centred * lax.rsqrt(row_var + 1e-05) * norm_gain + norm_bias).astype(bf16)
    width = full_rows.shape[1]
    head_width = w_qkv.shape[2]
    heads = head_width // HD
    qkv = jnp.dot(
        normed, w_qkv.reshape(width, 3 * head_width), preferred_element_type=f32
    ).astype(bf16)
    qkv = qkv.reshape(tiles, patches, 3, heads, HD)
    scores = jnp.einsum(
        "sqhe,skhe->shqk", qkv[:, :, 0], qkv[:, :, 1], preferred_element_type=f32
    ) / math.sqrt(HD)
    weights = jax.nn.softmax(scores, axis=-1).astype(bf16)
    context = jnp.einsum(
        "shqk,skhe->sqhe", weights, qkv[:, :, 2], preferred_element_type=f32
    ).astype(bf16)

    destination = route[:, 0]
    dest_hot = (destination[:, None] == jnp.arange(peers)[None, :]).astype(jnp.int32)
    earlier = jnp.cumsum(dest_hot, axis=0) - dest_hot
    position = jnp.sum(earlier * dest_hot, axis=1)
    target = destination * cap + position
    placing = target[:, None] == jnp.arange(peers * cap)[None, :]
    place_t = placing.astype(bf16).T
    occupied = jnp.sum(placing.astype(jnp.int32), axis=0).reshape(peers, 1, cap)
    occupied = jnp.broadcast_to(occupied, (peers, 1, cap))

    def send(values):
        rows = jnp.dot(
            place_t, values.reshape(tiles, patches * local_width), preferred_element_type=f32
        ).astype(bf16).reshape(peers, cap, patches * local_width)
        rows = lax.all_to_all(rows, "dp", split_axis=0, concat_axis=0, tiled=True)
        rows = lax.all_to_all(rows, "mp", split_axis=0, concat_axis=0, tiled=True)
        rows = rows.reshape(models, cap * patches, local_width)
        return rows.transpose(1, 0, 2).reshape(cap * patches, models * local_width)

    filled = lax.all_to_all(occupied, "dp", split_axis=0, concat_axis=0, tiled=True)
    used = lax.dynamic_index_in_dim(filled, lax.axis_index("mp"), 0, keepdims=False)[0] > 0
    ctx = send(context)
    emb = send(embedded)
    attended = jnp.dot(ctx, out_all, preferred_element_type=f32)
    encoded = (emb.astype(f32) + attended).astype(bf16)
    projected = lax.dot_general(
        encoded, w_all, (((1,), (1,)), ((), ())), preferred_element_type=f32
    )
    rows = cap * patches
    key_part = projected[:, :KVD].reshape(rows, KVD // DEC_HD, DEC_HD)
    key_scale = lax.rsqrt(jnp.mean(key_part * key_part, axis=-1, keepdims=True) + 1e-06)
    key_part = (key_part * key_scale * key_gain).reshape(rows, KVD)
    finished = jnp.concatenate([key_part, projected[:, KVD:]], axis=1)
    finished = finished.reshape(cap, patches, projected.shape[1])
    finished = jnp.where(used[:, None, None], finished, 0.0)
    return finished.astype(bf16)


N = 4
MESH = pl.DeviceIdType.MESH


def selector():
    table = np.zeros((N * HD, N * 128), np.float32)
    for head in range(N):
        for e in range(HD):
            table[head * HD + e, head * 128 + e] = 1.0
    return table


def kernel(
    emb_ref, trow_ref, gain_ref, bias_ref, wqkv_ref, wout_ref, wproj_ref, wkv_ref, kgain_ref,
    sel_ref, selt_ref, out_ref,
    embf, asrc, abuf, encg, fin, rssrc, rsbuf, own, wall,
    es, er, as_s, as_r, rs_s, rs_r, zs, zr, ys, yr, xs, xr, c_s, c_r, gs, gr, fs, fr,
):
    f32, bf16 = jnp.float32, jnp.bfloat16
    g, j, m = lax.axis_index("groups"), lax.axis_index("dp"), lax.axis_index("mp")
    xp = lax.rem(m + 2, N)
    cp = m + 1 - 2 * lax.rem(m, 2)
    xcp = lax.rem(cp + 2, N)
    rows, lanes = emb_ref.shape
    blk = wqkv_ref.shape[2]
    slots = out_ref.shape[0]
    half = wall.shape[3]

    def copy(src, dst, ssem, rsem, dev):
        return pltpu.make_async_remote_copy(
            src_ref=src, dst_ref=dst, send_sem=ssem, recv_sem=rsem,
            device_id=dev, device_id_type=MESH,
        )

    barrier = pltpu.get_barrier_semaphore()
    for k in range(1, N * N):
        other = lax.rem(j * N + m + k, N * N)
        pl.semaphore_signal(
            barrier, inc=1, device_id=(g, other // N, lax.rem(other, N)), device_id_type=MESH
        )
    pl.semaphore_signal(barrier, inc=1, device_id=(1 - g, j, m), device_id_type=MESH)
    pl.semaphore_wait(barrier, N * N)

    pending = []

    def start(c):
        c.start()
        pending.append(c)

    start(copy(emb_ref, embf.at[m], es.at[0], er.at[m], (g, j, xp)))
    start(copy(emb_ref, embf.at[m], es.at[1], er.at[m], (g, j, cp)))

    cols = pl.ds(pl.multiple_of(g * half, half), half)
    for k in (2, 3, 1, 0):
        to = lax.rem(m + k, N)
        prod = jnp.dot(
            wproj_ref[pl.ds(pl.multiple_of(to * blk, 16), blk), :], wkv_ref[:, cols],
            preferred_element_type=f32,
        )
        if k == 0:
            own[...] = prod
        else:
            rssrc[k] = prod.astype(bf16)
            start(copy(rssrc.at[k], rsbuf.at[m], rs_s.at[k], rs_r.at[m], (g, j, to)))

    embf[m] = emb_ref[...]

    copy(emb_ref, embf.at[xp], es.at[0], er.at[xp], (g, j, xp)).wait_recv()
    start(copy(embf.at[xp], embf.at[xp], es.at[2], er.at[xp], (g, j, cp)))

    total = own[...]
    for k in (1, 3, 2):
        frm = lax.rem(m + k, N)
        copy(rssrc.at[k], rsbuf.at[frm], rs_s.at[k], rs_r.at[frm], (g, j, frm)).wait_recv()
        total = total + rsbuf[frm].astype(f32)
    mine = pl.ds(pl.multiple_of(m * blk, 16), blk)
    xrow = pl.ds(pl.multiple_of(xp * blk, 16), blk)
    crow = pl.ds(pl.multiple_of(cp * blk, 16), blk)
    xcrow = pl.ds(pl.multiple_of(xcp * blk, 16), blk)
    wall[g, j, mine, :] = total.astype(bf16)
    unit = wall.at[g, j, mine, :]
    for k in (1, 3, 2):
        start(copy(unit, unit, zs.at[k], zr.at[j], (g, lax.rem(j + k, N), m)))

    def spread(gg, jj, at, across=True):
        u = wall.at[gg, jj, mine, :]
        if across:
            start(copy(u, u, xs.at[at], xr.at[gg, jj], (g, j, xp)))
        start(copy(u, u, c_s.at[at], c_r.at[gg, jj], (g, j, cp)))

    start(copy(unit, unit, ys.at[0], yr.at[j], (1 - g, j, m)))
    spread(g, j, 0)

    for b in (cp, xcp):
        copy(emb_ref, embf.at[b], es.at[0], er.at[b], (g, j, xp)).wait_recv()

    tile = rows // 16
    step = 4 * tile
    rid = lax.broadcasted_iota(jnp.int32, (step, step), 0) // tile
    cid = lax.broadcasted_iota(jnp.int32, (step, step), 1) // tile
    same = rid == cid

    def encode(r):
        at = pl.ds(pl.multiple_of(r * step, step), step)
        x = [embf[n, at, :][:, :blk].astype(f32) for n in range(N)]
        mean = sum(jnp.sum(v, axis=-1, keepdims=True) for v in x) / (N * blk)
        x = [v - mean for v in x]
        var = sum(jnp.sum(v * v, axis=-1, keepdims=True) for v in x) / (N * blk)
        inv = lax.rsqrt(var + 1e-05)
        x = [(x[n] * inv * gain_ref[n] + bias_ref[n]).astype(bf16) for n in range(N)]
        parts = []
        for k in range(3):
            acc = jnp.zeros((step, blk), f32)
            for n in range(N):
                acc = acc + jnp.dot(
                    x[n], wqkv_ref[k, n * blk:(n + 1) * blk, :], preferred_element_type=f32
                )
            parts.append(
                jnp.dot(acc.astype(bf16), sel_ref[...], preferred_element_type=f32).astype(bf16)
            )
        ctx = jnp.zeros((step, blk), f32)
        for h in range(N):
            hs = slice(h * 128, (h + 1) * 128)
            scores = lax.dot_general(
                parts[0][:, hs], parts[1][:, hs], (((1,), (1,)), ((), ())),
                preferred_element_type=f32,
            ) / math.sqrt(HD)
            scores = jnp.where(same, scores, -1e30)
            top = jnp.max(scores, axis=-1, keepdims=True)
            e = jnp.where(same, jnp.exp(scores - top), 0.0)
            wts = (e / jnp.sum(e, axis=-1, keepdims=True)).astype(bf16)
            c = jnp.dot(wts, parts[2][:, hs], preferred_element_type=f32).astype(bf16)
            ctx = ctx + jnp.dot(c, selt_ref[h * 128:(h + 1) * 128, :], preferred_element_type=f32)
        return jnp.dot(ctx.astype(bf16), wout_ref[...], preferred_element_type=f32)

    order = (0, 1, 3, 2)
    for k in (2, 3, 1):
        to = lax.rem(m + k, N)
        asrc[k] = encode(to).astype(bf16)
        start(copy(asrc.at[k], abuf.at[m], as_s.at[k], as_r.at[m], (g, j, to)))
        if k != 2:
            zk = 4 - k
            jj = lax.rem(j + zk, N)
            u = wall.at[g, jj, mine, :]
            copy(u, u, zs.at[zk], zr.at[jj], (g, j, xp)).wait_recv()
            start(copy(u, u, ys.at[zk], yr.at[jj], (1 - g, j, m)))
            spread(g, jj, zk)
    total = encode(m)
    jj = lax.rem(j + 2, N)
    u = wall.at[g, jj, mine, :]
    copy(u, u, zs.at[2], zr.at[jj], (g, j, xp)).wait_recv()
    start(copy(u, u, ys.at[2], yr.at[jj], (1 - g, j, m)))
    spread(g, jj, 2)

    for k in (1, 3, 2):
        frm = lax.rem(m + k, N)
        copy(asrc.at[k], abuf.at[frm], as_s.at[k], as_r.at[frm], (g, j, frm)).wait_recv()
        total = total + abuf[frm].astype(f32)
    at = pl.ds(pl.multiple_of(m * step, step), step)
    rows_own = jnp.concatenate([embf[n, at, :][:, :blk].astype(f32) for n in range(N)], axis=1)
    encg[j, :step, :] = (rows_own + total).astype(bf16)
    encg[j, step:, :] = trow_ref[...]
    for k in (2, 1, 3):
        start(copy(encg.at[j], encg.at[j], gs.at[k], gr.at[j], (g, lax.rem(j + k, N), m)))

    for k in order:
        jj = lax.rem(j + k, N)
        u = wall.at[1 - g, jj, mine, :]
        copy(u, u, ys.at[k], yr.at[jj], (1 - g, j, m)).wait_recv()
        spread(1 - g, jj, N + k, k < 2)

    for k in (1, 3, 2):
        frm = lax.rem(j + k, N)
        copy(encg.at[j], encg.at[frm], gs.at[k], gr.at[frm], (g, frm, m)).wait_recv()
    for k in (2, 3, 1):
        to = lax.rem(m + k, N)
        start(copy(encg.at[to], fin.at[m], fs.at[k], fr.at[m], (g, j, to)))
    fin[m] = encg[m]

    units = [(gg, k) for gg in range(2) for k in order]
    for gg, k in units:
        ga = g if gg == 0 else 1 - g
        jj = lax.rem(j + k, N)
        u = wall.at[ga, jj, xrow, :]
        copy(u, u, xs.at[gg * N + k], xr.at[ga, jj], (g, j, xp)).wait_recv()
        start(copy(u, u, c_s.at[8 + gg * N + k], c_r.at[2 + ga, jj], (g, j, cp)))
        if gg == 0 and k >= 2:
            start(copy(u, u, xs.at[N + k], xr.at[g, jj], (1 - g, j, m)))

    place = (lax.broadcasted_iota(jnp.int32, (slots, step), 0) + j * slots).astype(f32)
    patch = lax.rem(lax.broadcasted_iota(jnp.int32, (1, step), 1), tile).astype(f32)
    acc = jnp.zeros((slots, N * blk), f32)
    count = jnp.zeros((slots, 1), f32)
    for k in (0, 1, 3, 2):
        frm = lax.rem(m + k, N)
        if k:
            copy(encg.at[j], fin.at[frm], fs.at[k], fr.at[frm], (g, j, frm)).wait_recv()
        goal = fin[frm, step:, :][:1, :step].astype(f32) * tile + patch
        hot = (place == goal).astype(f32)
        count = count + jnp.sum(hot, axis=-1, keepdims=True)
        acc = acc + jnp.dot(hot.astype(bf16), fin[frm, :step, :], preferred_element_type=f32)
    enc = acc.astype(bf16)
    used = count > 0.5

    for gg, k in units:
        ga = g if gg == 0 else 1 - g
        jj = lax.rem(j + k, N)
        for b, row in ((0, crow), (2, xcrow)):
            u = wall.at[ga, jj, row, :]
            copy(u, u, c_s.at[0], c_r.at[b + ga, jj], (g, j, cp)).wait_recv()
        acc = jnp.dot(enc, wall[ga, jj], preferred_element_type=f32)
        key = (2 * jj + ga) * half < KVD
        for s in range(half // DEC_HD):
            p = acc[:, s * DEC_HD:(s + 1) * DEC_HD]
            scale = lax.rsqrt(jnp.mean(p * p, axis=-1, keepdims=True) + 1e-06)
            p = jnp.where(key, p * scale * kgain_ref[...], p)
            p = jnp.where(used, p, 0.0).astype(bf16)
            at = pl.ds(pl.multiple_of((2 * jj + ga) * half + s * DEC_HD, DEC_HD), DEC_HD)
            out_ref[:, at] = p

    for c in pending:
        c.wait_send()


def per_device_kernel(
    tile_rows, tile_count, tile_order, route, tile_embed, norm_gain, norm_bias,
    w_qkv, w_out, w_proj, w_kv, key_gain,
):
    f32, bf16 = jnp.float32, jnp.bfloat16
    tiles, patches, blk = tile_rows.shape
    cap = 2 * tiles // N
    rows, slots = tiles * patches, cap * patches
    width, columns = w_proj.shape[0], w_kv.shape[1] * N
    half = w_kv.shape[1] // 2
    lanes = -(-(blk + 1) // 128) * 128
    lookup = (tile_count - 1) * MAXT + tile_order
    lookup_hot = (lookup[:, None] == jnp.arange(MAXT * MAXT)[None, :]).astype(bf16)
    table_rows = jnp.dot(lookup_hot, tile_embed, preferred_element_type=f32)
    emb = (tile_rows.astype(f32) + table_rows[:, None, :]).astype(bf16).reshape(rows, blk)
    emb = jnp.pad(emb, ((0, 0), (0, lanes - blk)), constant_values=1)
    destination = route[:, 0]
    dest_hot = (destination[:, None] == jnp.arange(N)[None, :]).astype(jnp.int32)
    earlier = jnp.cumsum(dest_hot, axis=0) - dest_hot
    target = destination * cap + jnp.sum(earlier * dest_hot, axis=1)
    per = tiles // N
    trow = jnp.repeat(target.reshape(N, per), patches, axis=1)
    trow = lax.dynamic_slice_in_dim(trow, lax.axis_index("mp"), 1, 0).astype(bf16)
    trow = jnp.broadcast_to(jnp.pad(trow, ((0, 0), (0, width - per * patches))), (16, width))
    wqkv = w_qkv.transpose(1, 0, 2)
    sel = jnp.asarray(selector(), bf16)
    selt = jnp.asarray(selector().T, bf16)
    vm = pl.BlockSpec(memory_space=pltpu.VMEM)
    sem = pltpu.SemaphoreType.DMA
    out = pl.pallas_call(
        kernel,
        out_shape=jax.ShapeDtypeStruct((slots, columns), bf16),
        in_specs=[vm] * 11,
        out_specs=vm,
        scratch_shapes=[
            pltpu.VMEM((N, rows, lanes), bf16),
            pltpu.VMEM((N, rows // N, width), bf16),
            pltpu.VMEM((N, rows // N, width), bf16),
            pltpu.VMEM((N, rows // N + 16, width), bf16),
            pltpu.VMEM((N, rows // N + 16, width), bf16),
            pltpu.VMEM((N, blk, half), bf16),
            pltpu.VMEM((N, blk, half), bf16),
            pltpu.VMEM((blk, half), f32),
            pltpu.VMEM((2, N, width, half), bf16),
            sem((3,)), sem((N,)), sem((N,)), sem((N,)),
            sem((N,)), sem((N,)), sem((N,)), sem((N,)), sem((N,)), sem((N,)),
            sem((2 * N,)), sem((2, N)), sem((4 * N,)), sem((4, N)),
            sem((N,)), sem((N,)), sem((N,)), sem((N,)),
        ],
        compiler_params=pltpu.CompilerParams(
            collective_id=0, has_side_effects=True, vmem_limit_bytes=56 << 20
        ),
    )(
        emb, trow, norm_gain.reshape(N, 1, blk), norm_bias.reshape(N, 1, blk), wqkv, w_out,
        w_proj, w_kv, key_gain.reshape(1, -1), sel, selt,
    )
    return out.reshape(cap, patches, columns)


def solution(mesh):
    aligned = mesh.shape["dp"] == N and mesh.shape["mp"] == N and mesh.shape["groups"] == 2
    return jax.shard_map(
        per_device_kernel if aligned else per_device,
        mesh=mesh,
        in_specs=(
            P(("groups", "dp"), None, "mp"),
            P(("groups", "dp")),
            P(("groups", "dp")),
            P(("groups", "dp"), None),
            P(None, "mp"),
            P(),
            P(),
            P(None, None, "mp"),
            P("mp", None),
            P(None, "mp"),
            P("mp", "dp"),
            P(),
        ),
        out_specs=P(("groups", "dp", "mp"), None, None),
        check_vma=False,
    )
```

```python
import math

import jax
import jax.numpy as jnp
import numpy as np
from jax import lax
from jax.experimental import pallas as pl
from jax.experimental.pallas import tpu as pltpu
from jax.sharding import PartitionSpec as P

HD = 80
KVD = 1024
DEC_HD = 128
MAXT = 4


def per_device(
    tile_rows,
    tile_count,
    tile_order,
    route,
    tile_embed,
    norm_gain,
    norm_bias,
    w_qkv,
    w_out,
    w_proj,
    w_kv,
    key_gain,
):
    tiles, patches, local_width = tile_rows.shape
    peers = lax.axis_size("dp")
    models = lax.axis_size("mp")
    cap = 2 * tiles // peers
    f32, bf16 = jnp.float32, jnp.bfloat16

    part = lax.dot_general(w_kv, w_proj, (((0,), (1,)), ((), ())), preferred_element_type=f32)
    part = lax.psum_scatter(part.astype(bf16), "mp", scatter_dimension=0, tiled=True)
    w_all = lax.all_gather(part, ("dp", "mp"), axis=0, tiled=True)
    out_all = lax.all_gather(w_out, "mp", axis=0, tiled=True)

    lookup = (tile_count - 1) * MAXT + tile_order
    lookup_hot = (lookup[:, None] == jnp.arange(MAXT * MAXT)[None, :]).astype(bf16)
    table_rows = jnp.dot(lookup_hot, tile_embed, preferred_element_type=f32)
    embedded = (tile_rows.astype(f32) + table_rows[:, None, :]).astype(bf16)
    full_rows = lax.all_gather(
        embedded.reshape(tiles * patches, local_width), "mp", axis=1, tiled=True
    )
    full_float = full_rows.astype(f32)
    row_mean = jnp.mean(full_float, axis=-1, keepdims=True)
    centred = full_float - row_mean
    row_var = jnp.mean(centred * centred, axis=-1, keepdims=True)
    normed = (centred * lax.rsqrt(row_var + 1e-05) * norm_gain + norm_bias).astype(bf16)
    width = full_rows.shape[1]
    head_width = w_qkv.shape[2]
    heads = head_width // HD
    qkv = jnp.dot(
        normed, w_qkv.reshape(width, 3 * head_width), preferred_element_type=f32
    ).astype(bf16)
    qkv = qkv.reshape(tiles, patches, 3, heads, HD)
    scores = jnp.einsum(
        "sqhe,skhe->shqk", qkv[:, :, 0], qkv[:, :, 1], preferred_element_type=f32
    ) / math.sqrt(HD)
    weights = jax.nn.softmax(scores, axis=-1).astype(bf16)
    context = jnp.einsum(
        "shqk,skhe->sqhe", weights, qkv[:, :, 2], preferred_element_type=f32
    ).astype(bf16)

    destination = route[:, 0]
    dest_hot = (destination[:, None] == jnp.arange(peers)[None, :]).astype(jnp.int32)
    earlier = jnp.cumsum(dest_hot, axis=0) - dest_hot
    position = jnp.sum(earlier * dest_hot, axis=1)
    target = destination * cap + position
    placing = target[:, None] == jnp.arange(peers * cap)[None, :]
    place_t = placing.astype(bf16).T
    occupied = jnp.sum(placing.astype(jnp.int32), axis=0).reshape(peers, 1, cap)
    occupied = jnp.broadcast_to(occupied, (peers, 1, cap))

    def send(values):
        rows = jnp.dot(
            place_t, values.reshape(tiles, patches * local_width), preferred_element_type=f32
        ).astype(bf16).reshape(peers, cap, patches * local_width)
        rows = lax.all_to_all(rows, "dp", split_axis=0, concat_axis=0, tiled=True)
        rows = lax.all_to_all(rows, "mp", split_axis=0, concat_axis=0, tiled=True)
        rows = rows.reshape(models, cap * patches, local_width)
        return rows.transpose(1, 0, 2).reshape(cap * patches, models * local_width)

    filled = lax.all_to_all(occupied, "dp", split_axis=0, concat_axis=0, tiled=True)
    used = lax.dynamic_index_in_dim(filled, lax.axis_index("mp"), 0, keepdims=False)[0] > 0
    ctx = send(context)
    emb = send(embedded)
    attended = jnp.dot(ctx, out_all, preferred_element_type=f32)
    encoded = (emb.astype(f32) + attended).astype(bf16)
    projected = lax.dot_general(
        encoded, w_all, (((1,), (1,)), ((), ())), preferred_element_type=f32
    )
    rows = cap * patches
    key_part = projected[:, :KVD].reshape(rows, KVD // DEC_HD, DEC_HD)
    key_scale = lax.rsqrt(jnp.mean(key_part * key_part, axis=-1, keepdims=True) + 1e-06)
    key_part = (key_part * key_scale * key_gain).reshape(rows, KVD)
    finished = jnp.concatenate([key_part, projected[:, KVD:]], axis=1)
    finished = finished.reshape(cap, patches, projected.shape[1])
    finished = jnp.where(used[:, None, None], finished, 0.0)
    return finished.astype(bf16)


N = 4
MESH = pl.DeviceIdType.MESH


def selector():
    table = np.zeros((N * HD, N * 128), np.float32)
    for head in range(N):
        for e in range(HD):
            table[head * HD + e, head * 128 + e] = 1.0
    return table


def kernel(
    emb_ref, trow_ref, gain_ref, bias_ref, wqkv_ref, wout_ref, wproj_ref, wkv_ref, kgain_ref,
    sel_ref, selt_ref, out_ref,
    embf, asrc, abuf, encg, fin, rssrc, rsbuf, own, wall,
    es, er, as_s, as_r, rs_s, rs_r, zs, zr, ys, yr, xs, xr, c_s, c_r, gs, gr, fs, fr,
):
    f32, bf16 = jnp.float32, jnp.bfloat16
    g, j, m = lax.axis_index("groups"), lax.axis_index("dp"), lax.axis_index("mp")
    xp = lax.rem(m + 2, N)
    cp = m + 1 - 2 * lax.rem(m, 2)
    xcp = lax.rem(cp + 2, N)
    rows, lanes = emb_ref.shape
    blk = wqkv_ref.shape[2]
    slots = out_ref.shape[0]
    half = wall.shape[3]

    def copy(src, dst, ssem, rsem, dev):
        return pltpu.make_async_remote_copy(
            src_ref=src, dst_ref=dst, send_sem=ssem, recv_sem=rsem,
            device_id=dev, device_id_type=MESH,
        )

    barrier = pltpu.get_barrier_semaphore()
    for k in range(1, N * N):
        other = lax.rem(j * N + m + k, N * N)
        pl.semaphore_signal(
            barrier, inc=1, device_id=(g, other // N, lax.rem(other, N)), device_id_type=MESH
        )
    pl.semaphore_signal(barrier, inc=1, device_id=(1 - g, j, m), device_id_type=MESH)
    pl.semaphore_wait(barrier, N * N)

    pending = []

    def start(c):
        c.start()
        pending.append(c)

    start(copy(emb_ref, embf.at[m], es.at[0], er.at[m], (g, j, xp)))
    start(copy(emb_ref, embf.at[m], es.at[1], er.at[m], (g, j, cp)))

    cols = pl.ds(pl.multiple_of(g * half, half), half)
    for k in (2, 3, 1, 0):
        to = lax.rem(m + k, N)
        prod = jnp.dot(
            wproj_ref[pl.ds(pl.multiple_of(to * blk, 16), blk), :], wkv_ref[:, cols],
            preferred_element_type=f32,
        )
        if k == 0:
            own[...] = prod
        else:
            rssrc[k] = prod.astype(bf16)
            start(copy(rssrc.at[k], rsbuf.at[m], rs_s.at[k], rs_r.at[m], (g, j, to)))

    embf[m] = emb_ref[...]

    copy(emb_ref, embf.at[xp], es.at[0], er.at[xp], (g, j, xp)).wait_recv()
    start(copy(embf.at[xp], embf.at[xp], es.at[2], er.at[xp], (g, j, cp)))

    total = own[...]
    for k in (1, 3, 2):
        frm = lax.rem(m + k, N)
        copy(rssrc.at[k], rsbuf.at[frm], rs_s.at[k], rs_r.at[frm], (g, j, frm)).wait_recv()
        total = total + rsbuf[frm].astype(f32)
    mine = pl.ds(pl.multiple_of(m * blk, 16), blk)
    xrow = pl.ds(pl.multiple_of(xp * blk, 16), blk)
    crow = pl.ds(pl.multiple_of(cp * blk, 16), blk)
    xcrow = pl.ds(pl.multiple_of(xcp * blk, 16), blk)
    wall[g, j, mine, :] = total.astype(bf16)
    unit = wall.at[g, j, mine, :]
    for k in (1, 3, 2):
        start(copy(unit, unit, zs.at[k], zr.at[j], (g, lax.rem(j + k, N), m)))

    def spread(gg, jj, at, across=True):
        u = wall.at[gg, jj, mine, :]
        if across:
            start(copy(u, u, xs.at[at], xr.at[gg, jj], (g, j, xp)))
        start(copy(u, u, c_s.at[at], c_r.at[gg, jj], (g, j, cp)))

    start(copy(unit, unit, ys.at[0], yr.at[j], (1 - g, j, m)))
    spread(g, j, 0)

    for b in (cp, xcp):
        copy(emb_ref, embf.at[b], es.at[0], er.at[b], (g, j, xp)).wait_recv()

    tile = rows // 16
    step = 4 * tile
    rid = lax.broadcasted_iota(jnp.int32, (step, step), 0) // tile
    cid = lax.broadcasted_iota(jnp.int32, (step, step), 1) // tile
    same = rid == cid

    def encode(r):
        at = pl.ds(pl.multiple_of(r * step, step), step)
        x = [embf[n, at, :][:, :blk].astype(f32) for n in range(N)]
        mean = sum(jnp.sum(v, axis=-1, keepdims=True) for v in x) / (N * blk)
        x = [v - mean for v in x]
        var = sum(jnp.sum(v * v, axis=-1, keepdims=True) for v in x) / (N * blk)
        inv = lax.rsqrt(var + 1e-05)
        x = [(x[n] * inv * gain_ref[:, n * blk:(n + 1) * blk] + bias_ref[:, n * blk:(n + 1) * blk]).astype(bf16) for n in range(N)]
        parts = []
        for k in range(3):
            acc = jnp.zeros((step, blk), f32)
            for n in range(N):
                acc = acc + jnp.dot(
                    x[n], wqkv_ref[k, n * blk:(n + 1) * blk, :], preferred_element_type=f32
                )
            parts.append(
                jnp.dot(acc.astype(bf16), sel_ref[...], preferred_element_type=f32).astype(bf16)
            )
        ctx = jnp.zeros((step, blk), f32)
        for h in range(N):
            hs = slice(h * 128, (h + 1) * 128)
            scores = lax.dot_general(
                parts[0][:, hs], parts[1][:, hs], (((1,), (1,)), ((), ())),
                preferred_element_type=f32,
            ) / math.sqrt(HD)
            scores = jnp.where(same, scores, -1e30)
            top = jnp.max(scores, axis=-1, keepdims=True)
            e = jnp.where(same, jnp.exp(scores - top), 0.0)
            wts = (e / jnp.sum(e, axis=-1, keepdims=True)).astype(bf16)
            c = jnp.dot(wts, parts[2][:, hs], preferred_element_type=f32).astype(bf16)
            ctx = ctx + jnp.dot(c, selt_ref[h * 128:(h + 1) * 128, :], preferred_element_type=f32)
        return jnp.dot(ctx.astype(bf16), wout_ref[...], preferred_element_type=f32)

    order = (0, 1, 3, 2)
    for k in (2, 3, 1):
        to = lax.rem(m + k, N)
        asrc[k] = encode(to).astype(bf16)
        start(copy(asrc.at[k], abuf.at[m], as_s.at[k], as_r.at[m], (g, j, to)))
        if k != 2:
            zk = 4 - k
            jj = lax.rem(j + zk, N)
            u = wall.at[g, jj, mine, :]
            copy(u, u, zs.at[zk], zr.at[jj], (g, j, xp)).wait_recv()
            start(copy(u, u, ys.at[zk], yr.at[jj], (1 - g, j, m)))
            spread(g, jj, zk)
    total = encode(m)
    jj = lax.rem(j + 2, N)
    u = wall.at[g, jj, mine, :]
    copy(u, u, zs.at[2], zr.at[jj], (g, j, xp)).wait_recv()
    start(copy(u, u, ys.at[2], yr.at[jj], (1 - g, j, m)))
    spread(g, jj, 2)

    for k in (1, 3, 2):
        frm = lax.rem(m + k, N)
        copy(asrc.at[k], abuf.at[frm], as_s.at[k], as_r.at[frm], (g, j, frm)).wait_recv()
        total = total + abuf[frm].astype(f32)
    at = pl.ds(pl.multiple_of(m * step, step), step)
    rows_own = jnp.concatenate([embf[n, at, :][:, :blk].astype(f32) for n in range(N)], axis=1)
    encg[j, :step, :] = (rows_own + total).astype(bf16)
    encg[j, step:, :] = trow_ref[...]
    for k in (2, 1, 3):
        start(copy(encg.at[j], encg.at[j], gs.at[k], gr.at[j], (g, lax.rem(j + k, N), m)))

    for k in order:
        jj = lax.rem(j + k, N)
        u = wall.at[1 - g, jj, mine, :]
        copy(u, u, ys.at[k], yr.at[jj], (1 - g, j, m)).wait_recv()
        spread(1 - g, jj, N + k, False)

    units = [(gg, k) for gg in range(2) for k in order]

    def pass_on(gg):
        for k in order:
            ga = g if gg == 0 else 1 - g
            jj = lax.rem(j + k, N)
            u = wall.at[ga, jj, xrow, :]
            copy(u, u, xs.at[gg * N + k], xr.at[ga, jj], (g, j, xp)).wait_recv()
            if gg == 0:
                start(copy(u, u, xs.at[N + k], xr.at[g, jj], (1 - g, j, m)))
            start(copy(u, u, c_s.at[8 + gg * N + k], c_r.at[2 + ga, jj], (g, j, cp)))

    pass_on(0)

    for k in (1, 3, 2):
        frm = lax.rem(j + k, N)
        copy(encg.at[j], encg.at[frm], gs.at[k], gr.at[frm], (g, frm, m)).wait_recv()
    for k in (2, 3, 1):
        to = lax.rem(m + k, N)
        start(copy(encg.at[to], fin.at[m], fs.at[k], fr.at[m], (g, j, to)))
    fin[m] = encg[m]

    pass_on(1)

    place = (lax.broadcasted_iota(jnp.int32, (slots, step), 0) + j * slots).astype(f32)
    patch = lax.rem(lax.broadcasted_iota(jnp.int32, (1, step), 1), tile).astype(f32)
    acc = jnp.zeros((slots, N * blk), f32)
    count = jnp.zeros((slots, 1), f32)
    for k in (0, 1, 3, 2):
        frm = lax.rem(m + k, N)
        if k:
            copy(encg.at[j], fin.at[frm], fs.at[k], fr.at[frm], (g, j, frm)).wait_recv()
        goal = fin[frm, step:, :][:1, :step].astype(f32) * tile + patch
        hot = (place == goal).astype(f32)
        count = count + jnp.sum(hot, axis=-1, keepdims=True)
        acc = acc + jnp.dot(hot.astype(bf16), fin[frm, :step, :], preferred_element_type=f32)
    enc = acc.astype(bf16)
    used = count > 0.5

    for gg, k in units:
        ga = g if gg == 0 else 1 - g
        jj = lax.rem(j + k, N)
        for b, row in ((0, crow), (2, xcrow)):
            u = wall.at[ga, jj, row, :]
            copy(u, u, c_s.at[0], c_r.at[b + ga, jj], (g, j, cp)).wait_recv()
        acc = jnp.dot(enc, wall[ga, jj], preferred_element_type=f32)
        key = (2 * jj + ga) * half < KVD
        for s in range(half // DEC_HD):
            p = acc[:, s * DEC_HD:(s + 1) * DEC_HD]
            scale = lax.rsqrt(jnp.mean(p * p, axis=-1, keepdims=True) + 1e-06)
            p = jnp.where(key, p * scale * kgain_ref[...], p)
            p = jnp.where(used, p, 0.0).astype(bf16)
            at = pl.ds(pl.multiple_of((2 * jj + ga) * half + s * DEC_HD, DEC_HD), DEC_HD)
            out_ref[:, at] = p

    for c in pending:
        c.wait_send()


def per_device_kernel(
    tile_rows, tile_count, tile_order, route, tile_embed, norm_gain, norm_bias,
    w_qkv, w_out, w_proj, w_kv, key_gain,
):
    f32, bf16 = jnp.float32, jnp.bfloat16
    tiles, patches, blk = tile_rows.shape
    cap = 2 * tiles // N
    rows, slots = tiles * patches, cap * patches
    width, columns = w_proj.shape[0], w_kv.shape[1] * N
    half = w_kv.shape[1] // 2
    lookup = (tile_count - 1) * MAXT + tile_order
    lookup_hot = (lookup[:, None] == jnp.arange(MAXT * MAXT)[None, :]).astype(bf16)
    table_rows = jnp.dot(lookup_hot, tile_embed, preferred_element_type=f32)
    emb = (tile_rows.astype(f32) + table_rows[:, None, :]).astype(bf16).reshape(rows, blk)
    destination = route[:, 0]
    dest_hot = (destination[:, None] == jnp.arange(N)[None, :]).astype(jnp.int32)
    earlier = jnp.cumsum(dest_hot, axis=0) - dest_hot
    target = destination * cap + jnp.sum(earlier * dest_hot, axis=1)
    per = tiles // N
    trow = jnp.repeat(target.reshape(N, per), patches, axis=1)
    trow = lax.dynamic_slice_in_dim(trow, lax.axis_index("mp"), 1, 0).astype(bf16)
    trow = jnp.broadcast_to(jnp.pad(trow, ((0, 0), (0, width - per * patches))), (16, width))
    wqkv = w_qkv.transpose(1, 0, 2)
    sel = jnp.asarray(selector(), bf16)
    selt = jnp.asarray(selector().T, bf16)
    vm = pl.BlockSpec(memory_space=pltpu.VMEM)
    sem = pltpu.SemaphoreType.DMA
    out = pl.pallas_call(
        kernel,
        out_shape=jax.ShapeDtypeStruct((slots, columns), bf16),
        in_specs=[vm] * 11,
        out_specs=vm,
        scratch_shapes=[
            pltpu.VMEM((N, rows, blk), bf16),
            pltpu.VMEM((N, rows // N, width), bf16),
            pltpu.VMEM((N, rows // N, width), bf16),
            pltpu.VMEM((N, rows // N + 16, width), bf16),
            pltpu.VMEM((N, rows // N + 16, width), bf16),
            pltpu.VMEM((N, blk, half), bf16),
            pltpu.VMEM((N, blk, half), bf16),
            pltpu.VMEM((blk, half), f32),
            pltpu.VMEM((2, N, width, half), bf16),
            sem((3,)), sem((N,)), sem((N,)), sem((N,)),
            sem((N,)), sem((N,)), sem((N,)), sem((N,)), sem((N,)), sem((N,)),
            sem((2 * N,)), sem((2, N)), sem((4 * N,)), sem((4, N)),
            sem((N,)), sem((N,)), sem((N,)), sem((N,)),
        ],
        compiler_params=pltpu.CompilerParams(
            collective_id=0, has_side_effects=True, vmem_limit_bytes=56 << 20
        ),
    )(
        emb, trow, norm_gain.reshape(1, width), norm_bias.reshape(1, width), wqkv, w_out,
        w_proj, w_kv, key_gain.reshape(1, -1), sel, selt,
    )
    return out.reshape(cap, patches, columns)


def solution(mesh):
    aligned = mesh.shape["dp"] == N and mesh.shape["mp"] == N and mesh.shape["groups"] == 2
    return jax.shard_map(
        per_device_kernel if aligned else per_device,
        mesh=mesh,
        in_specs=(
            P(("groups", "dp"), None, "mp"),
            P(("groups", "dp")),
            P(("groups", "dp")),
            P(("groups", "dp"), None),
            P(None, "mp"),
            P(),
            P(),
            P(None, None, "mp"),
            P("mp", None),
            P(None, "mp"),
            P("mp", "dp"),
            P(),
        ),
        out_specs=P(("groups", "dp", "mp"), None, None),
        check_vma=False,
    )
```

```python
import math

import jax
import jax.numpy as jnp
import numpy as np
from jax import lax
from jax.experimental import pallas as pl
from jax.experimental.pallas import tpu as pltpu
from jax.sharding import PartitionSpec as P

HD = 80
KVD = 1024
DEC_HD = 128
MAXT = 4


def per_device(
    tile_rows,
    tile_count,
    tile_order,
    route,
    tile_embed,
    norm_gain,
    norm_bias,
    w_qkv,
    w_out,
    w_proj,
    w_kv,
    key_gain,
):
    tiles, patches, local_width = tile_rows.shape
    peers = lax.axis_size("dp")
    models = lax.axis_size("mp")
    cap = 2 * tiles // peers
    f32, bf16 = jnp.float32, jnp.bfloat16

    part = lax.dot_general(w_kv, w_proj, (((0,), (1,)), ((), ())), preferred_element_type=f32)
    part = lax.psum_scatter(part.astype(bf16), "mp", scatter_dimension=0, tiled=True)
    w_all = lax.all_gather(part, ("dp", "mp"), axis=0, tiled=True)
    out_all = lax.all_gather(w_out, "mp", axis=0, tiled=True)

    lookup = (tile_count - 1) * MAXT + tile_order
    lookup_hot = (lookup[:, None] == jnp.arange(MAXT * MAXT)[None, :]).astype(bf16)
    table_rows = jnp.dot(lookup_hot, tile_embed, preferred_element_type=f32)
    embedded = (tile_rows.astype(f32) + table_rows[:, None, :]).astype(bf16)
    full_rows = lax.all_gather(
        embedded.reshape(tiles * patches, local_width), "mp", axis=1, tiled=True
    )
    full_float = full_rows.astype(f32)
    row_mean = jnp.mean(full_float, axis=-1, keepdims=True)
    centred = full_float - row_mean
    row_var = jnp.mean(centred * centred, axis=-1, keepdims=True)
    normed = (centred * lax.rsqrt(row_var + 1e-05) * norm_gain + norm_bias).astype(bf16)
    width = full_rows.shape[1]
    head_width = w_qkv.shape[2]
    heads = head_width // HD
    qkv = jnp.dot(
        normed, w_qkv.reshape(width, 3 * head_width), preferred_element_type=f32
    ).astype(bf16)
    qkv = qkv.reshape(tiles, patches, 3, heads, HD)
    scores = jnp.einsum(
        "sqhe,skhe->shqk", qkv[:, :, 0], qkv[:, :, 1], preferred_element_type=f32
    ) / math.sqrt(HD)
    weights = jax.nn.softmax(scores, axis=-1).astype(bf16)
    context = jnp.einsum(
        "shqk,skhe->sqhe", weights, qkv[:, :, 2], preferred_element_type=f32
    ).astype(bf16)

    destination = route[:, 0]
    dest_hot = (destination[:, None] == jnp.arange(peers)[None, :]).astype(jnp.int32)
    earlier = jnp.cumsum(dest_hot, axis=0) - dest_hot
    position = jnp.sum(earlier * dest_hot, axis=1)
    target = destination * cap + position
    placing = target[:, None] == jnp.arange(peers * cap)[None, :]
    place_t = placing.astype(bf16).T
    occupied = jnp.sum(placing.astype(jnp.int32), axis=0).reshape(peers, 1, cap)
    occupied = jnp.broadcast_to(occupied, (peers, 1, cap))

    def send(values):
        rows = jnp.dot(
            place_t, values.reshape(tiles, patches * local_width), preferred_element_type=f32
        ).astype(bf16).reshape(peers, cap, patches * local_width)
        rows = lax.all_to_all(rows, "dp", split_axis=0, concat_axis=0, tiled=True)
        rows = lax.all_to_all(rows, "mp", split_axis=0, concat_axis=0, tiled=True)
        rows = rows.reshape(models, cap * patches, local_width)
        return rows.transpose(1, 0, 2).reshape(cap * patches, models * local_width)

    filled = lax.all_to_all(occupied, "dp", split_axis=0, concat_axis=0, tiled=True)
    used = lax.dynamic_index_in_dim(filled, lax.axis_index("mp"), 0, keepdims=False)[0] > 0
    ctx = send(context)
    emb = send(embedded)
    attended = jnp.dot(ctx, out_all, preferred_element_type=f32)
    encoded = (emb.astype(f32) + attended).astype(bf16)
    projected = lax.dot_general(
        encoded, w_all, (((1,), (1,)), ((), ())), preferred_element_type=f32
    )
    rows = cap * patches
    key_part = projected[:, :KVD].reshape(rows, KVD // DEC_HD, DEC_HD)
    key_scale = lax.rsqrt(jnp.mean(key_part * key_part, axis=-1, keepdims=True) + 1e-06)
    key_part = (key_part * key_scale * key_gain).reshape(rows, KVD)
    finished = jnp.concatenate([key_part, projected[:, KVD:]], axis=1)
    finished = finished.reshape(cap, patches, projected.shape[1])
    finished = jnp.where(used[:, None, None], finished, 0.0)
    return finished.astype(bf16)


N = 4
MESH = pl.DeviceIdType.MESH


def selector():
    table = np.zeros((N * HD, N * 128), np.float32)
    for head in range(N):
        for e in range(HD):
            table[head * HD + e, head * 128 + e] = 1.0
    return table


def kernel(
    emb_ref, trow_ref, norm_ref, wqkv_ref, wout_ref, wproj_ref, wkv_ref, kgain_ref,
    sel_ref, selt_ref, out_ref,
    embf, asrc, abuf, encg, fin, rssrc, rsbuf, own, wall,
    es, er, as_s, as_r, rs_s, rs_r, zs, zr, ys, yr, xs, xr, c_s, c_r, gs, gr, fs, fr,
):
    f32, bf16 = jnp.float32, jnp.bfloat16
    g, j, m = lax.axis_index("groups"), lax.axis_index("dp"), lax.axis_index("mp")
    xp = lax.rem(m + 2, N)
    cp = m + 1 - 2 * lax.rem(m, 2)
    xcp = lax.rem(cp + 2, N)
    rows, lanes = emb_ref.shape
    blk = wqkv_ref.shape[2]
    slots = out_ref.shape[0]
    half = wall.shape[3]

    def copy(src, dst, ssem, rsem, dev):
        return pltpu.make_async_remote_copy(
            src_ref=src, dst_ref=dst, send_sem=ssem, recv_sem=rsem,
            device_id=dev, device_id_type=MESH,
        )

    barrier = pltpu.get_barrier_semaphore()
    for k in range(1, N * N):
        other = lax.rem(j * N + m + k, N * N)
        pl.semaphore_signal(
            barrier, inc=1, device_id=(g, other // N, lax.rem(other, N)), device_id_type=MESH
        )
    pl.semaphore_signal(barrier, inc=1, device_id=(1 - g, j, m), device_id_type=MESH)
    pl.semaphore_wait(barrier, N * N)

    pending = []

    def start(c):
        c.start()
        pending.append(c)

    start(copy(emb_ref, embf.at[m], es.at[0], er.at[m], (g, j, xp)))
    start(copy(emb_ref, embf.at[m], es.at[1], er.at[m], (g, j, cp)))

    cols = pl.ds(pl.multiple_of(g * half, half), half)
    for k in (2, 3, 1, 0):
        to = lax.rem(m + k, N)
        prod = jnp.dot(
            wproj_ref[pl.ds(pl.multiple_of(to * blk, 16), blk), :], wkv_ref[:, cols],
            preferred_element_type=f32,
        )
        if k == 0:
            own[...] = prod
        else:
            rssrc[k] = prod.astype(bf16)
            start(copy(rssrc.at[k], rsbuf.at[m], rs_s.at[k], rs_r.at[m], (g, j, to)))

    embf[m] = emb_ref[...]

    copy(emb_ref, embf.at[xp], es.at[0], er.at[xp], (g, j, xp)).wait_recv()
    start(copy(embf.at[xp], embf.at[xp], es.at[2], er.at[xp], (g, j, cp)))

    total = own[...]
    for k in (1, 3, 2):
        frm = lax.rem(m + k, N)
        copy(rssrc.at[k], rsbuf.at[frm], rs_s.at[k], rs_r.at[frm], (g, j, frm)).wait_recv()
        total = total + rsbuf[frm].astype(f32)
    mine = pl.ds(pl.multiple_of(m * blk, 16), blk)
    xrow = pl.ds(pl.multiple_of(xp * blk, 16), blk)
    crow = pl.ds(pl.multiple_of(cp * blk, 16), blk)
    xcrow = pl.ds(pl.multiple_of(xcp * blk, 16), blk)
    wall[g, j, mine, :] = total.astype(bf16)
    unit = wall.at[g, j, mine, :]
    for k in (1, 3, 2):
        start(copy(unit, unit, zs.at[k], zr.at[j], (g, lax.rem(j + k, N), m)))

    def spread(gg, jj, at, across=True):
        u = wall.at[gg, jj, mine, :]
        if across:
            start(copy(u, u, xs.at[at], xr.at[gg, jj], (g, j, xp)))
        start(copy(u, u, c_s.at[at], c_r.at[gg, jj], (g, j, cp)))

    start(copy(unit, unit, ys.at[0], yr.at[j], (1 - g, j, m)))
    spread(g, j, 0)

    for b in (cp, xcp):
        copy(emb_ref, embf.at[b], es.at[0], er.at[b], (g, j, xp)).wait_recv()

    tile = rows // 16
    step = 4 * tile
    rid = lax.broadcasted_iota(jnp.int32, (step, step), 0) // tile
    cid = lax.broadcasted_iota(jnp.int32, (step, step), 1) // tile
    same = rid == cid

    def encode(r):
        at = pl.ds(pl.multiple_of(r * step, step), step)
        x = [embf[n, at, :][:, :blk].astype(f32) for n in range(N)]
        mean = sum(jnp.sum(v, axis=-1, keepdims=True) for v in x) / (N * blk)
        x = [v - mean for v in x]
        var = sum(jnp.sum(v * v, axis=-1, keepdims=True) for v in x) / (N * blk)
        inv = lax.rsqrt(var + 1e-05)
        x = [(x[n] * inv * norm_ref[0:1, n * blk:(n + 1) * blk] + norm_ref[1:2, n * blk:(n + 1) * blk]).astype(bf16) for n in range(N)]
        parts = []
        for k in range(3):
            acc = jnp.zeros((step, blk), f32)
            for n in range(N):
                acc = acc + jnp.dot(
                    x[n], wqkv_ref[k, n * blk:(n + 1) * blk, :], preferred_element_type=f32
                )
            parts.append(
                jnp.dot(acc.astype(bf16), sel_ref[...], preferred_element_type=f32).astype(bf16)
            )
        ctx = jnp.zeros((step, blk), f32)
        for h in range(N):
            hs = slice(h * 128, (h + 1) * 128)
            scores = lax.dot_general(
                parts[0][:, hs], parts[1][:, hs], (((1,), (1,)), ((), ())),
                preferred_element_type=f32,
            ) / math.sqrt(HD)
            scores = jnp.where(same, scores, -1e30)
            top = jnp.max(scores, axis=-1, keepdims=True)
            e = jnp.where(same, jnp.exp(scores - top), 0.0)
            wts = (e / jnp.sum(e, axis=-1, keepdims=True)).astype(bf16)
            c = jnp.dot(wts, parts[2][:, hs], preferred_element_type=f32).astype(bf16)
            ctx = ctx + jnp.dot(c, selt_ref[h * 128:(h + 1) * 128, :], preferred_element_type=f32)
        return jnp.dot(ctx.astype(bf16), wout_ref[...], preferred_element_type=f32)

    order = (0, 1, 3, 2)
    for k in (2, 3, 1):
        to = lax.rem(m + k, N)
        asrc[k] = encode(to).astype(bf16)
        start(copy(asrc.at[k], abuf.at[m], as_s.at[k], as_r.at[m], (g, j, to)))
        if k != 2:
            zk = 4 - k
            jj = lax.rem(j + zk, N)
            u = wall.at[g, jj, mine, :]
            copy(u, u, zs.at[zk], zr.at[jj], (g, j, xp)).wait_recv()
            start(copy(u, u, ys.at[zk], yr.at[jj], (1 - g, j, m)))
            spread(g, jj, zk)
    total = encode(m)
    jj = lax.rem(j + 2, N)
    u = wall.at[g, jj, mine, :]
    copy(u, u, zs.at[2], zr.at[jj], (g, j, xp)).wait_recv()
    start(copy(u, u, ys.at[2], yr.at[jj], (1 - g, j, m)))
    spread(g, jj, 2)

    for k in (1, 3, 2):
        frm = lax.rem(m + k, N)
        copy(asrc.at[k], abuf.at[frm], as_s.at[k], as_r.at[frm], (g, j, frm)).wait_recv()
        total = total + abuf[frm].astype(f32)
    at = pl.ds(pl.multiple_of(m * step, step), step)
    rows_own = jnp.concatenate([embf[n, at, :][:, :blk].astype(f32) for n in range(N)], axis=1)
    encg[j, :step, :] = (rows_own + total).astype(bf16)
    encg[j, step:, :] = trow_ref[...]
    for k in (2, 1, 3):
        start(copy(encg.at[j], encg.at[j], gs.at[k], gr.at[j], (g, lax.rem(j + k, N), m)))

    for k in order:
        jj = lax.rem(j + k, N)
        u = wall.at[1 - g, jj, mine, :]
        copy(u, u, ys.at[k], yr.at[jj], (1 - g, j, m)).wait_recv()
        spread(1 - g, jj, N + k, False)

    units = [(gg, k) for gg in range(2) for k in order]

    def pass_on(gg):
        for k in order:
            ga = g if gg == 0 else 1 - g
            jj = lax.rem(j + k, N)
            u = wall.at[ga, jj, xrow, :]
            copy(u, u, xs.at[gg * N + k], xr.at[ga, jj], (g, j, xp)).wait_recv()
            if gg == 0:
                start(copy(u, u, xs.at[N + k], xr.at[g, jj], (1 - g, j, m)))
            start(copy(u, u, c_s.at[8 + gg * N + k], c_r.at[2 + ga, jj], (g, j, cp)))

    pass_on(0)

    for k in (1, 3, 2):
        frm = lax.rem(j + k, N)
        copy(encg.at[j], encg.at[frm], gs.at[k], gr.at[frm], (g, frm, m)).wait_recv()
    for k in (2, 3, 1):
        to = lax.rem(m + k, N)
        start(copy(encg.at[to], fin.at[m], fs.at[k], fr.at[m], (g, j, to)))
    fin[m] = encg[m]

    pass_on(1)

    place = (lax.broadcasted_iota(jnp.int32, (slots, step), 0) + j * slots).astype(f32)
    patch = lax.rem(lax.broadcasted_iota(jnp.int32, (1, step), 1), tile).astype(f32)
    acc = jnp.zeros((slots, N * blk), f32)
    count = jnp.zeros((slots, 1), f32)
    for k in (0, 1, 3, 2):
        frm = lax.rem(m + k, N)
        if k:
            copy(encg.at[j], fin.at[frm], fs.at[k], fr.at[frm], (g, j, frm)).wait_recv()
        goal = fin[frm, step:, :][:1, :step].astype(f32) * tile + patch
        hot = (place == goal).astype(f32)
        count = count + jnp.sum(hot, axis=-1, keepdims=True)
        acc = acc + jnp.dot(hot.astype(bf16), fin[frm, :step, :], preferred_element_type=f32)
    enc = acc.astype(bf16)
    used = count > 0.5

    for gg, k in units:
        ga = g if gg == 0 else 1 - g
        jj = lax.rem(j + k, N)
        for b, row in ((0, crow), (2, xcrow)):
            u = wall.at[ga, jj, row, :]
            copy(u, u, c_s.at[0], c_r.at[b + ga, jj], (g, j, cp)).wait_recv()
        acc = jnp.dot(enc, wall[ga, jj], preferred_element_type=f32)
        key = (2 * jj + ga) * half < KVD
        for s in range(half // DEC_HD):
            p = acc[:, s * DEC_HD:(s + 1) * DEC_HD]
            scale = lax.rsqrt(jnp.mean(p * p, axis=-1, keepdims=True) + 1e-06)
            p = jnp.where(key, p * scale * kgain_ref[...], p)
            p = jnp.where(used, p, 0.0).astype(bf16)
            at = pl.ds(pl.multiple_of((2 * jj + ga) * half + s * DEC_HD, DEC_HD), DEC_HD)
            out_ref[:, at] = p

    for c in pending:
        c.wait_send()


def per_device_kernel(
    tile_rows, tile_count, tile_order, route, tile_embed, norm_gain, norm_bias,
    w_qkv, w_out, w_proj, w_kv, key_gain,
):
    f32, bf16 = jnp.float32, jnp.bfloat16
    tiles, patches, blk = tile_rows.shape
    cap = 2 * tiles // N
    rows, slots = tiles * patches, cap * patches
    width, columns = w_proj.shape[0], w_kv.shape[1] * N
    half = w_kv.shape[1] // 2
    lookup = (tile_count - 1) * MAXT + tile_order
    lookup_hot = (lookup[:, None] == jnp.arange(MAXT * MAXT)[None, :]).astype(bf16)
    table_rows = jnp.dot(lookup_hot, tile_embed, preferred_element_type=f32)
    emb = (tile_rows.astype(f32) + table_rows[:, None, :]).astype(bf16).reshape(rows, blk)
    destination = route[:, 0]
    dest_hot = (destination[:, None] == jnp.arange(N)[None, :]).astype(jnp.int32)
    earlier = jnp.cumsum(dest_hot, axis=0) - dest_hot
    target = destination * cap + jnp.sum(earlier * dest_hot, axis=1)
    per = tiles // N
    trow = jnp.repeat(target.reshape(N, per), patches, axis=1)
    trow = lax.dynamic_slice_in_dim(trow, lax.axis_index("mp"), 1, 0).astype(bf16)
    trow = jnp.broadcast_to(jnp.pad(trow, ((0, 0), (0, width - per * patches))), (16, width))
    wqkv = w_qkv.transpose(1, 0, 2)
    sel = jnp.asarray(selector(), bf16)
    selt = jnp.asarray(selector().T, bf16)
    vm = pl.BlockSpec(memory_space=pltpu.VMEM)
    sem = pltpu.SemaphoreType.DMA
    out = pl.pallas_call(
        kernel,
        out_shape=jax.ShapeDtypeStruct((slots, columns), bf16),
        in_specs=[vm] * 10,
        out_specs=vm,
        scratch_shapes=[
            pltpu.VMEM((N, rows, blk), bf16),
            pltpu.VMEM((N, rows // N, width), bf16),
            pltpu.VMEM((N, rows // N, width), bf16),
            pltpu.VMEM((N, rows // N + 16, width), bf16),
            pltpu.VMEM((N, rows // N + 16, width), bf16),
            pltpu.VMEM((N, blk, half), bf16),
            pltpu.VMEM((N, blk, half), bf16),
            pltpu.VMEM((blk, half), f32),
            pltpu.VMEM((2, N, width, half), bf16),
            sem((3,)), sem((N,)), sem((N,)), sem((N,)),
            sem((N,)), sem((N,)), sem((N,)), sem((N,)), sem((N,)), sem((N,)),
            sem((2 * N,)), sem((2, N)), sem((4 * N,)), sem((4, N)),
            sem((N,)), sem((N,)), sem((N,)), sem((N,)),
        ],
        compiler_params=pltpu.CompilerParams(
            collective_id=0, has_side_effects=True, vmem_limit_bytes=56 << 20
        ),
    )(
        emb, trow, jnp.stack([norm_gain, norm_bias]), wqkv, w_out,
        w_proj, w_kv, key_gain.reshape(1, -1), sel, selt,
    )
    return out.reshape(cap, patches, columns)


def solution(mesh):
    aligned = mesh.shape["dp"] == N and mesh.shape["mp"] == N and mesh.shape["groups"] == 2
    return jax.shard_map(
        per_device_kernel if aligned else per_device,
        mesh=mesh,
        in_specs=(
            P(("groups", "dp"), None, "mp"),
            P(("groups", "dp")),
            P(("groups", "dp")),
            P(("groups", "dp"), None),
            P(None, "mp"),
            P(),
            P(),
            P(None, None, "mp"),
            P("mp", None),
            P(None, "mp"),
            P("mp", "dp"),
            P(),
        ),
        out_specs=P(("groups", "dp", "mp"), None, None),
        check_vma=False,
    )
```
